512 devices in a mesh: prompt: 4 (over x), ctx: 128 (over z, y, core).
Axes of the slice: x: 4, y: 8, z: 8, core: 2. Of those that a mesh axis runs over, the one named last changes fastest.
Arguments:
- queries: bfloat16 [4, 512, 32, 128], P('prompt', 'ctx'), may hold values from -8 to 8
- prefix_keys: bfloat16 [4, 32768, 2, 128], P('prompt', 'ctx'), may hold values from -16 to 16
- prompt_value_rows: bfloat16 [4, 32768, 2, 128], P('prompt', 'ctx'), may hold values from -6 to 6
- generated_keys: bfloat16 [4, 512, 32, 2, 128], P('prompt', 'ctx'), may hold values from -16 to 16
- generated_values: bfloat16 [4, 512, 32, 2, 128], P('prompt', 'ctx'), may hold values from -6 to 6
- suffix_lengths: int32 [4, 512], P('prompt', 'ctx'), may hold values from 1 to 32, as said below
- hidden_rows: bfloat16 [4, 512, 2048], P('prompt', 'ctx'), may hold values from -6 to 6
- routed_experts: int32 [512, 4, 8], P('ctx'), may hold values from 0 to 127, all different within a row; in each aligned block of 16 rows (0 to 15, 16 to 31, ..., all dimensions but the last counted through in order) at most 2 rows name the same one
- routing_weights: float32 [512, 4, 8], P('ctx'), may hold values from 0.05 to 0.3
- gate_weight: bfloat16 [128, 768, 2048], P('ctx', 'prompt'), may hold values from -0.125 to 0.125
- up_weight: bfloat16 [128, 768, 2048], P('ctx', 'prompt'), may hold values from -0.125 to 0.125
- down_weight: bfloat16 [128, 768, 2048], P('ctx', 'prompt'), may hold values from -0.21875 to 0.21875
Outputs:
- attended: bfloat16 [4, 512, 32, 128], P('prompt', 'ctx')
- expert_mix: bfloat16 [4, 512, 2048], P('prompt', 'ctx')
The draws below stay inside these ranges and needn't reach their ends.
Inputs may be any that keep to these rules, and one draw needn't show every extreme that they name: `suffix_lengths`: some sample's suffix has exactly 32 live positions. `routed_experts`: each row names 8 different experts. In the rows of one index of ctx (aligned blocks of 16 rows, samples major), no expert is named by more than 2 rows, a bound that some block reaches.
All inputs are finite; a program needn't handle non-finite values.
Results may differ from the reference program's by a relative error of at most 0.013.
Values may be sent and summed in bfloat16 or wider, within the bound.
No kernel may reach another device: no remote copies, remote signals or barrier semaphores. Data moves between devices by JAX's collectives and lax.ppermute only.
A program may use at most 128 MiB of HBM per device.

```python
import math
import jax
import jax.numpy as jnp
import numpy as np
from jax import lax

D = 2048
FF = 768
HQ = 32
KEY_HEADS = 2
HEAD_WIDTH = 128
TOP = 8
SMP_DEV = 4
SUFFIX_LENGTH = 32
PROMPT_COUNT = 4
SAMPLE_TOTAL = 512
PROMPT_LENGTH = 32768
EXPERTS = 128
QUERY_PER_HEAD = 16
UNIT_PART = 192
CAP = 2
N_PROMPT = 4
N_CTX = 128


def draw_queries(key, part):
    key = jax.random.fold_in(key, 7)
    tensor_shape = (PROMPT_COUNT, SAMPLE_TOTAL, HQ, HEAD_WIDTH)
    drawn = jnp.clip(jax.random.normal(key, tensor_shape), -6.0, 6.0)
    return drawn.astype(jnp.bfloat16)


def draw_prefix_keys(key, part):
    key = jax.random.fold_in(key, 3)
    tensor_shape = (PROMPT_COUNT, PROMPT_LENGTH, KEY_HEADS, HEAD_WIDTH)
    drawn = jnp.clip(jax.random.normal(key, tensor_shape) * 2.2, -13.0, 13.0)
    return drawn.astype(jnp.bfloat16)


def draw_suffix_lengths(key, part):
    key = jax.random.fold_in(key, 5)
    length_key, prompt_key, sample_key = jax.random.split(key, 3)
    lengths = jax.random.randint(length_key, (PROMPT_COUNT, SAMPLE_TOTAL), 1, SUFFIX_LENGTH + 1)
    full_prompt = jax.random.randint(prompt_key, (), 0, PROMPT_COUNT)
    full_sample = jax.random.randint(sample_key, (), 0, SAMPLE_TOTAL)
    return lengths.at[full_prompt, full_sample].set(SUFFIX_LENGTH).astype(jnp.int32)


def block_levels(key, shape, shards, least, largest):
    def one(position, blocks):
        heights = jax.random.uniform(jax.random.fold_in(jax.random.fold_in(key, 6), position), (blocks,), jnp.float32, least / len(shards), largest / len(shards))
        return jnp.repeat(jnp.exp(heights), shape[position] // blocks).reshape((-1,) + (1,) * (len(shape) - position - 1))

    loudness = one(*shards[0])
    for cut in shards[1:]:
        loudness = loudness * one(*cut)
    return loudness


def routed_block(stream_key, own, number, rows, count, top, most, lean):
    sequence = jax.random.permutation(stream_key, count)
    packed, usual = portions_of(count, rows * top, most, lean, True), portions_of(count, rows * top, most, lean, False)
    places = jnp.arange(count)

    def named(tallies, turn):
        used = int((tallies > 0).sum())
        fixed = max(1, used // 4)
        passed = fixed + (places - fixed + turn * (used - fixed)) % max(1, count - fixed)
        return jnp.zeros((count,), jnp.int32).at[sequence[jnp.where(places < fixed, places, passed)]].set(jnp.asarray(tallies, jnp.int32))

    tallies = jnp.where(number % 4 == 0, named(packed, number // 4), named(usual, number - number // 4 - 1))
    mixed = jax.random.permutation(jax.random.fold_in(own, 3), count)
    source_of, receiver = mixed[0:count // 2 * 2:2], mixed[1:count // 2 * 2:2]
    margin = jnp.minimum(tallies[source_of] - 1, most - tallies[receiver]) // 2
    margin = jnp.where((source_of == sequence[0]) | (receiver == sequence[0]) | (tallies[receiver] == 0), 0, jnp.maximum(margin, 0))
    passed = jax.random.randint(jax.random.fold_in(own, 4), (count // 2,), 0, 1 << 20) % (margin + 1)
    tallies = tallies.at[source_of].add(-passed).at[receiver].add(passed)
    items = jnp.searchsorted(jnp.cumsum(tallies), jnp.arange(rows * top), side="right").astype(jnp.int32)
    grid = items.reshape(top, rows).T
    grid = grid[jax.random.permutation(jax.random.fold_in(own, 1), rows)]
    turn = jax.random.randint(jax.random.fold_in(own, 2), (rows, 1), 0, top)
    return jnp.take_along_axis(grid, (jnp.arange(top)[None, :] + turn) % top, axis=1)


def portions_of(amount, total, limit, skew, full):
    loads = [(1 << 20) // math.isqrt(standing ** skew) + 1 for standing in range(1, amount + 1)]
    largest = limit if full else min(limit, max(-(-total // amount), total * loads[0] // sum(loads)))
    least = 1 if total - largest >= amount - 1 else 0
    counts, spare = [largest] + [least] * (amount - 1), total - largest - least * (amount - 1)
    while spare > 0:
        free = [i for i in range(1, amount) if counts[i] < largest] or [i for i in range(1, amount) if counts[i] < limit]
        mass, remaining = sum([loads[i] for i in free]), spare
        for i in free:
            addition = min(limit - counts[i], max(1, remaining * loads[i] // mass), spare)
            counts[i] = counts[i] + addition
            spare = spare - addition
    return np.array(counts)


def gaussian(stream_key, dims, width, bound, cuts=(), kind=jnp.bfloat16):
    values = jax.random.normal(stream_key, dims, jnp.float32) * width
    if len(cuts) > 0:
        values = block_levels(stream_key, dims, cuts, -0.22, 0.18) * values
    return jnp.clip(values, min=-bound, max=bound).astype(kind)


def setup_inputs(seed: int = 0) -> dict:
    keys = jax.random.split(jax.random.key(seed), 13)
    queries = draw_queries(jax.random.fold_in(keys[12], 71), 0)
    prefix_keys = draw_prefix_keys(jax.random.fold_in(keys[12], 71), 0)
    prompt_value_rows = gaussian(keys[2], (PROMPT_COUNT, PROMPT_LENGTH, KEY_HEADS, HEAD_WIDTH), 1.0, 6.0, ((0, 4), (1, 128)))
    generated_keys = gaussian(keys[3], (PROMPT_COUNT, SAMPLE_TOTAL, SUFFIX_LENGTH, KEY_HEADS, HEAD_WIDTH), 3.8, 16.0, ((0, 4), (1, 128)))
    generated_values = gaussian(keys[4], (PROMPT_COUNT, SAMPLE_TOTAL, SUFFIX_LENGTH, KEY_HEADS, HEAD_WIDTH), 1.0, 6.0, ((0, 4), (1, 128)))
    suffix_lengths = draw_suffix_lengths(jax.random.fold_in(keys[12], 71), 0)
    hidden_rows = gaussian(keys[6], (PROMPT_COUNT, SAMPLE_TOTAL, D), 1.0, 6.0, ((0, 4), (1, 128)))
    routed_experts_keys = jax.random.split(jax.random.fold_in(keys[7], 1), SAMPLE_TOTAL * PROMPT_COUNT // (N_PROMPT * SMP_DEV))
    routed_experts_turns = jax.random.permutation(jax.random.fold_in(keys[7], 3), SAMPLE_TOTAL * PROMPT_COUNT // (N_PROMPT * SMP_DEV))
    routed_experts = jax.vmap(lambda own, number: routed_block(jax.random.fold_in(keys[7], 2), own, number, N_PROMPT * SMP_DEV, EXPERTS, TOP, CAP, 2))(routed_experts_keys, routed_experts_turns).reshape((SAMPLE_TOTAL, PROMPT_COUNT, TOP))
    routing_weights = jnp.clip(0.05 + 0.25 * jax.random.uniform(keys[8], (SAMPLE_TOTAL, PROMPT_COUNT, TOP), jnp.float32) ** block_levels(keys[8], (SAMPLE_TOTAL, PROMPT_COUNT, TOP), ((0, 128),), -0.2, 0.2), 0.05, 0.3)
    gate_weight = gaussian(keys[9], (EXPERTS, FF, D), D ** -0.5, 0.125, ((0, 128), (1, 4)))
    up_weight = gaussian(keys[10], (EXPERTS, FF, D), D ** -0.5, 0.125, ((0, 128), (1, 4)))
    down_weight = gaussian(keys[11], (EXPERTS, FF, D), FF ** -0.5, 0.21875, ((0, 128), (1, 4)))
    return dict(queries=queries, prefix_keys=prefix_keys, prompt_value_rows=prompt_value_rows, generated_keys=generated_keys, generated_values=generated_values, suffix_lengths=suffix_lengths, hidden_rows=hidden_rows, routed_experts=routed_experts, routing_weights=routing_weights, gate_weight=gate_weight, up_weight=up_weight, down_weight=down_weight)


def round_half(values_wide):
    narrow = values_wide.astype(jnp.bfloat16)
    narrow = lax.optimization_barrier(narrow)
    return narrow.astype(jnp.float32)


def row_product(left, right):
    return lax.dot_general(left, right, (((1,), (1,)), ((), ())), preferred_element_type=jnp.float32)


def attend_block(block_of_queries, key_cache, value_cache, trailing_keys, trailing_values, tail_lengths):
    rows_per_block = block_of_queries.shape[0]
    score_scale = HEAD_WIDTH ** -0.5
    broad_query = block_of_queries.astype(jnp.float32).reshape(rows_per_block, KEY_HEADS, QUERY_PER_HEAD, HEAD_WIDTH)
    prefix_scores = jnp.einsum("bgqd,tgd->bgqt", broad_query, key_cache) * score_scale
    suffix_scores = jnp.einsum("bgqd,bjgd->bgqj", broad_query, trailing_keys.astype(jnp.float32)) * score_scale
    active = (jnp.arange(SUFFIX_LENGTH)[None, :] < tail_lengths[:, None])[:, None, None, :]
    suffix_scores = jnp.where(active, suffix_scores, -1e30)
    peaks = jnp.maximum(jnp.max(prefix_scores, axis=3), jnp.max(suffix_scores, axis=3))
    prefix_terms = jnp.exp(prefix_scores - peaks[..., None])
    suffix_terms = jnp.where(active, jnp.exp(suffix_scores - peaks[..., None]), 0.0)
    totals = jnp.sum(prefix_terms, axis=3) + jnp.sum(suffix_terms, axis=3)
    numerator = jnp.einsum("bgqt,tgd->bgqd", round_half(prefix_terms), value_cache)
    numerator = numerator + jnp.einsum("bgqj,bjgd->bgqd", round_half(suffix_terms), trailing_values.astype(jnp.float32))
    return (numerator / totals[..., None]).reshape(rows_per_block, HQ, HEAD_WIDTH).astype(jnp.bfloat16)


def attend_prompt(prompt_inputs):
    prompt_queries, prompt_keys, prompt_values, trailing_keys, trailing_values, tail_lengths = prompt_inputs
    key_cache = prompt_keys.astype(jnp.float32)
    value_cache = prompt_values.astype(jnp.float32)
    rows_per_block = 8
    count_of_blocks = SAMPLE_TOTAL // rows_per_block
    grouped = (
        prompt_queries.reshape(count_of_blocks, rows_per_block, HQ, HEAD_WIDTH),
        trailing_keys.reshape(count_of_blocks, rows_per_block, SUFFIX_LENGTH, KEY_HEADS, HEAD_WIDTH),
        trailing_values.reshape(count_of_blocks, rows_per_block, SUFFIX_LENGTH, KEY_HEADS, HEAD_WIDTH),
        tail_lengths.reshape(count_of_blocks, rows_per_block),
    )
    result = lax.map(lambda block_inputs: attend_block(block_inputs[0], key_cache, value_cache, block_inputs[1], block_inputs[2], block_inputs[3]), grouped)
    return result.reshape(SAMPLE_TOTAL, HQ, HEAD_WIDTH)


def reference(queries, prefix_keys, prompt_value_rows, generated_keys, generated_values, suffix_lengths, hidden_rows, routed_experts, routing_weights, gate_weight, up_weight, down_weight):
    attended = lax.map(attend_prompt, (queries, prefix_keys, prompt_value_rows, generated_keys, generated_values, suffix_lengths))
    row_total = PROMPT_COUNT * SAMPLE_TOTAL
    most_rows = N_CTX * CAP
    row_matrix = hidden_rows.reshape(row_total, D)
    chosen = jnp.transpose(routed_experts, (1, 0, 2)).reshape(row_total, TOP)
    gate_share = jnp.transpose(routing_weights, (1, 0, 2)).reshape(row_total, TOP)

    def per_expert(accum, expert_inputs):
        expert, gate_matrix, up_matrix, down_matrix = expert_inputs
        matches = chosen == expert
        row_weight = jnp.sum(jnp.where(matches, gate_share, 0.0), axis=1)
        picked = jnp.nonzero(jnp.any(matches, axis=1), size=most_rows, fill_value=row_total)[0]
        safe_rows = jnp.minimum(picked, row_total - 1)
        inputs_block = row_matrix[safe_rows]
        gate_act = row_product(inputs_block, gate_matrix)
        up_act = row_product(inputs_block, up_matrix)
        activation = (jax.nn.silu(gate_act) * up_act).astype(jnp.bfloat16)
        pieces = jnp.einsum(
            "rqf,qfd->qrd",
            activation.reshape(most_rows, PROMPT_COUNT, UNIT_PART).astype(jnp.float32),
            down_matrix.reshape(PROMPT_COUNT, UNIT_PART, D).astype(jnp.float32),
        )
        summed = jnp.sum(round_half(pieces), axis=0)
        scale_rows = jnp.where(picked < row_total, row_weight[safe_rows], 0.0)
        accum = accum.at[picked].add(scale_rows[:, None] * summed, mode="drop")
        return accum, None

    start = jnp.zeros((row_total, D), jnp.float32)
    mixed, unused = lax.scan(per_expert, start, (jnp.arange(EXPERTS, dtype=jnp.int32), gate_weight, up_weight, down_weight))
    expert_mix = mixed.reshape(PROMPT_COUNT, SAMPLE_TOTAL, D).astype(jnp.bfloat16)
    return attended, expert_mix
```

```python
import math

import jax
import jax.numpy as jnp
from jax import lax
from jax.experimental import pallas as pl
from jax.experimental.pallas import tpu as pltpu
from jax.sharding import Mesh
from jax.sharding import PartitionSpec as P

BF16 = jnp.bfloat16
F32 = jnp.float32
LOG2E = 1.4426950408889634
EXTRA = 16


def three_parts(value):
    high = value.astype(BF16)
    rest = value - high.astype(F32)
    middle = rest.astype(BF16)
    low = (rest - middle.astype(F32)).astype(BF16)
    return high, middle, low


def attention_kernel(scale, q_ref, kv_ref, out_ref, vaug_ref):
    samples, groups, per_group, width = q_ref.shape
    dests = out_ref.shape[0]
    positions = kv_ref.shape[0] * kv_ref.shape[3]

    @pl.when(pl.program_id(0) == 0)
    def _():
        for g in range(groups):
            vaug_ref[g, :, :width] = kv_ref[:, 1, g].reshape(positions, width)
            vaug_ref[g, :, width:] = jnp.ones((positions, width), BF16)

    outs, logs = [], []
    for g in range(groups):
        rows = q_ref[:, g].reshape(samples * per_group, width)
        keys = kv_ref[:, 0, g].reshape(positions, width)
        scores = lax.dot_general(rows, keys, (((1,), (1,)), ((), ())), preferred_element_type=F32)
        peak = jnp.max(scores, axis=1, keepdims=True)
        probs = jnp.exp2((scores - peak) * (scale * LOG2E)).astype(BF16)
        summed = jnp.dot(probs, vaug_ref[g], preferred_element_type=F32)
        total = summed[:, width:]
        outs.append((summed[:, :width] / total).astype(BF16).reshape(samples, 1, per_group, width))
        logs.append((peak * scale + jnp.log(total)).reshape(samples, 1, per_group, width))
    out_ref[:, : groups * per_group * (samples // dests), :] = jnp.concatenate(outs, axis=1).reshape(
        dests, samples // dests * groups * per_group, width
    )
    joined = jnp.concatenate(logs, axis=1).reshape(dests, samples // dests * groups * per_group, width)
    for d in range(dests):
        line = jnp.transpose(joined[d])[0:1, :]
        parts = jnp.concatenate(
            [part.astype(F32) for part in three_parts(line)] + [jnp.zeros((EXTRA - 3, width), F32)], axis=0
        )
        out_ref[d, width:, :] = parts.astype(BF16)


def attention(q_all, kv_all, scale):
    sources, own, heads, width = q_all.shape
    groups = kv_all.shape[2]
    samples = sources * own
    dests_per_step = 4
    steps = sources // dests_per_step
    positions = kv_all.shape[0] * kv_all.shape[3]
    pairs = samples * heads * positions
    q_view = q_all.reshape(samples, groups, heads // groups, width)
    return pl.pallas_call(
        lambda *refs: attention_kernel(scale, *refs),
        grid=(steps,),
        in_specs=[
            pl.BlockSpec((samples // steps, groups, heads // groups, width), lambda i: (i, 0, 0, 0)),
            pl.BlockSpec(kv_all.shape, lambda i: (0, 0, 0, 0, 0)),
        ],
        out_specs=pl.BlockSpec((dests_per_step, own * heads + EXTRA, width), lambda i: (i, 0, 0)),
        out_shape=jax.ShapeDtypeStruct((sources, own * heads + EXTRA, width), BF16),
        scratch_shapes=[pltpu.VMEM((groups, positions, 2 * width), BF16)],
        compiler_params=pltpu.CompilerParams(vmem_limit_bytes=40 * 1024 * 1024),
        cost_estimate=pl.CostEstimate(
            flops=6 * pairs * width, bytes_accessed=2 * (kv_all.size + 2 * q_all.size), transcendentals=pairs
        ),
        name="prompt_attention",
    )(q_view, kv_all)


def expert_kernel(place_ref, piece0, piece1, piece2, piece3, gate_ref, up_ref, down_ref, *out_refs):
    parts = len(out_refs)
    width = piece0.shape[1]
    place = place_ref[0]
    gate = up = None
    for shift, piece in enumerate((piece0, piece1, piece2, piece3)):
        block = lax.rem(place - shift + parts, parts)
        columns = pl.ds(pl.multiple_of(block * width, width), width)
        dims = (((1,), (1,)), ((), ()))
        more_gate = lax.dot_general(piece[...], gate_ref[:, columns], dims, preferred_element_type=F32)
        more_up = lax.dot_general(piece[...], up_ref[:, columns], dims, preferred_element_type=F32)
        gate = more_gate if gate is None else gate + more_gate
        up = more_up if up is None else up + more_up
    act = (gate / (1.0 + jnp.exp(-gate)) * up).astype(BF16)
    for shift, out_ref in enumerate(out_refs):
        block = lax.rem(place + shift, parts)
        columns = pl.ds(pl.multiple_of(block * width, width), width)
        out_ref[...] = jnp.dot(act, down_ref[:, columns], preferred_element_type=F32).astype(BF16)


def expert_parts(place, pieces, gate_weight, up_weight, down_weight):
    rows, width = pieces[0].shape
    parts = len(pieces)
    vmem = pl.BlockSpec(memory_space=pltpu.VMEM)
    return pl.pallas_call(
        expert_kernel,
        in_specs=[pl.BlockSpec(memory_space=pltpu.SMEM)] + [vmem] * (parts + 3),
        out_specs=[vmem] * parts,
        out_shape=[jax.ShapeDtypeStruct((rows, width), BF16)] * parts,
        compiler_params=pltpu.CompilerParams(vmem_limit_bytes=24 * 1024 * 1024),
        cost_estimate=pl.CostEstimate(
            flops=6 * rows * width * parts * gate_weight.shape[0],
            bytes_accessed=6 * gate_weight.size + 16 * rows * width,
            transcendentals=rows * gate_weight.shape[0],
        ),
        name="expert_parts",
    )(place, *pieces, gate_weight, up_weight, down_weight)


def suffix_part(own_query, keys, values, lengths, scale):
    scores = jnp.einsum("bgqd,bjgd->bgqj", own_query, keys, preferred_element_type=F32) * scale
    live = (jnp.arange(keys.shape[1], dtype=jnp.int32)[None, :] < lengths[:, None])[:, None, None, :]
    scores = jnp.where(live, scores, -1e30)
    peak = jnp.max(scores, axis=3)
    terms = jnp.where(live, jnp.exp(scores - peak[..., None]), 0.0)
    total = jnp.sum(terms, axis=3)
    summed = jnp.einsum("bgqj,bjgd->bgqd", terms.astype(BF16), values, preferred_element_type=F32)
    return summed / total[..., None], peak + jnp.log(total)


def body(
    queries,
    prefix_keys,
    prompt_value_rows,
    generated_keys,
    generated_values,
    suffix_lengths,
    hidden_rows,
    routed_experts,
    routing_weights,
    gate_weight,
    up_weight,
    down_weight,
):
    prompts = lax.axis_size("x")
    place = lax.axis_index("x")
    own, heads, width = queries.shape[1:]
    groups = prefix_keys.shape[2]
    scale = width ** (-0.5)

    kv = jnp.stack([prefix_keys[0].transpose(1, 0, 2), prompt_value_rows[0].transpose(1, 0, 2)])
    kv_all = lax.all_gather(kv, "z", axis=0, tiled=False)
    q_all = lax.all_gather(queries[0], ("y", "c"), axis=0, tiled=False)

    features = hidden_rows.shape[2]
    quarter = features // prompts
    row_quarter = lax.all_to_all(
        hidden_rows.reshape(own, 1, features), "x", split_axis=2, concat_axis=1, tiled=True
    ).reshape(own * prompts, quarter)
    rows = own * prompts
    top = routed_experts.shape[2]
    experts = lax.axis_size(("z", "y", "c")) * gate_weight.shape[0]
    slots = min(2, rows)
    chosen = routed_experts.reshape(rows, top)
    shares = routing_weights.reshape(rows, top)
    matches = chosen[:, :, None] == jnp.arange(experts, dtype=jnp.int32)[None, None, :]
    named = jnp.any(matches, axis=1)
    share_of = jnp.sum(jnp.where(matches, shares[:, :, None], 0.0), axis=1)
    earlier = jnp.cumsum(named.astype(jnp.int32), axis=0) - named.astype(jnp.int32)
    slot_is = named[:, :, None] & (earlier[:, :, None] == jnp.arange(slots, dtype=jnp.int32)[None, None, :])
    sent = jnp.einsum("rej,rd->ejd", slot_is.astype(BF16), row_quarter, preferred_element_type=F32).astype(BF16)
    arrived = lax.all_to_all(sent, ("z", "y", "c"), split_axis=0, concat_axis=0, tiled=True)
    piece = arrived.reshape(experts * slots, quarter)
    pieces = [piece] + [
        lax.ppermute(piece, "x", [(i, (i + s) % prompts) for i in range(prompts)]) for s in range(1, prompts)
    ]
    parts = expert_parts(
        place.astype(jnp.int32).reshape(1), pieces, gate_weight[0], up_weight[0], down_weight[0]
    )
    received = [parts[0]] + [
        lax.ppermute(parts[s], "x", [(i, (i + s) % prompts) for i in range(prompts)]) for s in range(1, prompts)
    ]
    expert_sum = sum(r.astype(F32) for r in received).astype(BF16)
    returned = lax.all_to_all(
        expert_sum.reshape(experts, slots, quarter), ("z", "y", "c"), split_axis=0, concat_axis=0, tiled=True
    ).reshape(experts * slots, quarter)
    share_slots = jnp.where(slot_is, share_of[:, :, None], 0.0).reshape(rows, experts * slots)
    share_high = share_slots.astype(BF16)
    share_low = (share_slots - share_high.astype(F32)).astype(BF16)
    mixed = jnp.dot(jnp.concatenate([share_high, share_low]), returned, preferred_element_type=F32)
    mixed = (mixed[:rows] + mixed[rows:]).astype(BF16).reshape(own, prompts, quarter)
    expert_mix = lax.all_to_all(mixed, "x", split_axis=1, concat_axis=2, tiled=True).reshape(1, own, features)

    packed = attention(q_all, kv_all, scale)
    back = lax.all_to_all(packed, ("y", "c"), split_axis=0, concat_axis=0, tiled=True)
    suffix_out, suffix_log = suffix_part(
        queries[0].reshape(own, groups, heads // groups, width),
        generated_keys[0],
        generated_values[0],
        suffix_lengths[0],
        scale,
    )
    count = own * heads
    partial = back[:, :count].astype(F32)
    logs = jnp.sum(back[:, count : count + 3].astype(F32), axis=1)
    suffix_log = suffix_log.reshape(count)
    highest = jnp.maximum(jnp.max(logs, axis=0), suffix_log)
    weight = jnp.exp(logs - highest)
    suffix_weight = jnp.exp(suffix_log - highest)
    total = jnp.sum(weight, axis=0) + suffix_weight
    summed = jnp.sum(partial * weight[..., None], axis=0) + suffix_out.reshape(count, width) * suffix_weight[:, None]
    attended = (summed / total[:, None]).astype(BF16).reshape(1, own, heads, width)
    return attended, expert_mix


def solution(mesh):
    prompts = mesh.shape["prompt"]
    ctx = mesh.shape["ctx"]
    across = math.isqrt(ctx // 2)
    grid = Mesh(mesh.devices.reshape(prompts, across, across, 2), ("x", "z", "y", "c"))
    lay = ("z", "y", "c")
    placed = (
        P("x", lay, None, None),
        P("x", lay, None, None),
        P("x", lay, None, None),
        P("x", lay, None, None, None),
        P("x", lay, None, None, None),
        P("x", lay),
        P("x", lay, None),
        P(lay, None, None),
        P(lay, None, None),
        P(lay, "x", None),
        P(lay, "x", None),
        P(lay, "x", None),
    )
    return jax.shard_map(
        body,
        mesh=grid,
        in_specs=placed,
        out_specs=(P("x", lay, None, None), P("x", lay, None)),
        check_vma=False,
    )
```

```python
import functools
import math

import jax
import jax.numpy as jnp
from jax import lax
from jax.experimental import pallas as pl
from jax.experimental.pallas import tpu as pltpu
from jax.sharding import Mesh
from jax.sharding import PartitionSpec as P

BF16 = jnp.bfloat16
F32 = jnp.float32
LOG2E = 1.4426950408889634
NEAR = 4
SLOTS = 2
EXTRA = 16


def three_parts(value):
    high = value.astype(BF16)
    rest = value - high.astype(F32)
    middle = rest.astype(BF16)
    low = (rest - middle.astype(F32)).astype(BF16)
    return high, middle, low


def pack(out_ref, at, values, line):
    rows, width = values.shape
    parts = [part.astype(F32) for part in three_parts(line)]
    extra = jnp.concatenate(parts + [jnp.zeros((EXTRA - 3, width), F32)], axis=0).astype(BF16)
    at = at if isinstance(at, tuple) else (at,)
    out_ref[at + (slice(0, rows),)] = values.astype(BF16)
    out_ref[at + (slice(rows, rows + EXTRA),)] = extra


def unpack_line(ref, at, rows):
    logs = ref[at, rows:, :].astype(F32)
    return logs[0:1] + logs[1:2] + logs[2:3]


def attention_kernel(scale, *refs):
    q_refs, kv_ref, out_refs = refs[:NEAR], refs[NEAR], refs[NEAR + 1 : 2 * NEAR + 1]
    q_buf, k_buf, v_buf, vaug, out_buf, q_sem, kv_sem, out_sem = refs[2 * NEAR + 1 :]
    samples, groups, per_group, width = q_refs[0].shape
    dests = out_refs[0].shape[0]
    own = samples // dests
    positions = kv_ref.shape[0] * kv_ref.shape[3]
    q_in = [pltpu.make_async_copy(q_refs[i], q_buf.at[i], q_sem.at[i]) for i in range(NEAR)]
    k_in = [pltpu.make_async_copy(kv_ref.at[:, 0, g], k_buf.at[g], kv_sem.at[0, g]) for g in range(groups)]
    v_in = [pltpu.make_async_copy(kv_ref.at[:, 1, g], v_buf.at[g], kv_sem.at[1, g]) for g in range(groups)]
    out = [pltpu.make_async_copy(out_buf.at[i], out_refs[i], out_sem.at[i]) for i in range(NEAR)]
    for copy in q_in + k_in + v_in:
        copy.start()
    for g in range(groups):
        vaug[g, :, width:] = jnp.ones((positions, width), BF16)
    for copy in q_in + k_in + v_in:
        copy.wait()
    for g in range(groups):
        vaug[g, :, :width] = v_buf[g].reshape(positions, width)
    for first in (2, 0):
        outs, logs = [], []
        for g in range(groups):
            rows = jnp.concatenate(
                [q_buf[first + i, :, g].reshape(samples * per_group, width) for i in range(2)], axis=0
            )
            keys = k_buf[g].reshape(positions, width)
            scores = lax.dot_general(rows, keys, (((1,), (1,)), ((), ())), preferred_element_type=F32)
            peak = jnp.max(scores, axis=1, keepdims=True)
            probs = jnp.exp2((scores - peak) * (scale * LOG2E)).astype(BF16)
            summed = jnp.dot(probs, vaug[g], preferred_element_type=F32)
            total = summed[:, width:]
            outs.append((summed[:, :width] / total).reshape(2 * samples, 1, per_group, width))
            logs.append((peak * scale + jnp.log(total)).reshape(2 * samples, 1, per_group, width))
        shape = (2 * dests, own * groups * per_group, width)
        values = jnp.concatenate(outs, axis=1).reshape(shape)
        joined = jnp.concatenate(logs, axis=1).reshape(shape)
        for i in range(2):
            for d in range(dests):
                at = i * dests + d
                pack(out_buf, (first + i, d), values[at], jnp.transpose(joined[at])[0:1, :])
    for copy in out:
        copy.start()
    for copy in out:
        copy.wait()


def attention(q_parts, kv_all, scale):
    sources, own, heads, width = q_parts[0].shape
    groups = kv_all.shape[2]
    samples = sources * own
    positions = kv_all.shape[0] * kv_all.shape[3]
    pairs = NEAR * samples * heads * positions
    views = [q.reshape(samples, groups, heads // groups, width) for q in q_parts]
    part = jax.ShapeDtypeStruct((sources, own * heads + EXTRA, width), BF16)
    hbm = pl.BlockSpec(memory_space=pltpu.HBM)
    return pl.pallas_call(
        lambda *refs: attention_kernel(scale, *refs),
        in_specs=[hbm] * (NEAR + 1),
        out_specs=[hbm] * NEAR,
        out_shape=[part] * NEAR,
        scratch_shapes=[
            pltpu.VMEM((NEAR,) + views[0].shape, BF16),
            pltpu.VMEM((groups, kv_all.shape[0], kv_all.shape[3], width), BF16),
            pltpu.VMEM((groups, kv_all.shape[0], kv_all.shape[3], width), BF16),
            pltpu.VMEM((groups, positions, 2 * width), BF16),
            pltpu.VMEM((NEAR,) + part.shape, BF16),
            pltpu.SemaphoreType.DMA((NEAR,)),
            pltpu.SemaphoreType.DMA((2, groups)),
            pltpu.SemaphoreType.DMA((NEAR,)),
        ],
        compiler_params=pltpu.CompilerParams(vmem_limit_bytes=62 * 1024 * 1024),
        cost_estimate=pl.CostEstimate(
            flops=6 * pairs * width, bytes_accessed=2 * (kv_all.size + 8 * q_parts[0].size), transcendentals=pairs
        ),
        name="prompt_attention",
    )(*views, kv_all)


def merged(values, lines):
    highest = functools.reduce(jnp.maximum, lines)
    weights = [jnp.exp(line - highest) for line in lines]
    total = sum(weights)
    shape = values[0].shape
    result = sum(v * jnp.transpose(jnp.broadcast_to(w / total, shape)) for v, w in zip(values, weights, strict=True))
    return result, highest + jnp.log(total)


def merge_kernel(*refs):
    part_refs, keep_ref, send_ref = refs[:-2], refs[-2], refs[-1]
    rows = keep_ref.shape[2]
    for d, out_ref in ((1, send_ref), (0, keep_ref)):
        values, line = merged(
            [ref[d, :rows, :].astype(F32) for ref in part_refs], [unpack_line(ref, d, rows) for ref in part_refs]
        )
        pack(out_ref, 0, values, line)


def merge(parts):
    half = jax.ShapeDtypeStruct((parts[0].shape[0] // 2,) + parts[0].shape[1:], BF16)
    vmem = pl.BlockSpec(memory_space=pltpu.VMEM)
    size = parts[0].size
    return pl.pallas_call(
        merge_kernel,
        in_specs=[vmem] * len(parts),
        out_specs=[vmem] * 2,
        out_shape=[half] * 2,
        cost_estimate=pl.CostEstimate(flops=20 * size, bytes_accessed=10 * size, transcendentals=0),
        name="merge_partials",
    )(*parts)


def last_merge_kernel(mine_ref, other_ref, suffix_ref, suffix_log_ref, out_ref):
    rows = out_ref.shape[0]
    refs = (mine_ref, other_ref)
    values, _ = merged(
        [ref[0, :rows, :].astype(F32) for ref in refs] + [suffix_ref[...]],
        [unpack_line(ref, 0, rows) for ref in refs] + [suffix_log_ref[...]],
    )
    out_ref[...] = values.astype(BF16)


def last_merge(mine, other, suffix, suffix_log):
    vmem = pl.BlockSpec(memory_space=pltpu.VMEM)
    return pl.pallas_call(
        last_merge_kernel,
        in_specs=[vmem] * 4,
        out_specs=vmem,
        out_shape=jax.ShapeDtypeStruct(suffix.shape, BF16),
        cost_estimate=pl.CostEstimate(flops=20 * suffix.size, bytes_accessed=16 * suffix.size, transcendentals=0),
        name="last_merge",
    )(mine, other, suffix, suffix_log)


def expert_kernel(rows_ref, gate_ref, up_ref, down_ref, out_ref):
    parts, rows, width = rows_ref.shape
    dims = (((1,), (1,)), ((), ()))
    gate = up = None
    for part in range(parts):
        columns = slice(part * width, (part + 1) * width)
        piece = rows_ref[part]
        more_gate = lax.dot_general(piece, gate_ref[:, columns], dims, preferred_element_type=F32)
        more_up = lax.dot_general(piece, up_ref[:, columns], dims, preferred_element_type=F32)
        gate = more_gate if gate is None else gate + more_gate
        up = more_up if up is None else up + more_up
    act = (gate / (1.0 + jnp.exp(-gate)) * up).astype(BF16)
    for part in range(parts):
        columns = slice(part * width, (part + 1) * width)
        out_ref[part] = jnp.dot(act, down_ref[:, columns], preferred_element_type=F32).astype(BF16)


def expert_parts(pieces, gate_weight, up_weight, down_weight):
    parts, rows, width = pieces.shape
    vmem = pl.BlockSpec(memory_space=pltpu.VMEM)
    return pl.pallas_call(
        expert_kernel,
        in_specs=[vmem] * 4,
        out_specs=vmem,
        out_shape=jax.ShapeDtypeStruct(pieces.shape, BF16),
        compiler_params=pltpu.CompilerParams(vmem_limit_bytes=24 * 1024 * 1024),
        cost_estimate=pl.CostEstimate(
            flops=6 * rows * width * parts * gate_weight.shape[0],
            bytes_accessed=6 * gate_weight.size + 4 * pieces.size,
            transcendentals=rows * gate_weight.shape[0],
        ),
        name="expert_parts",
    )(pieces, gate_weight, up_weight, down_weight)


def local_kernel(
    scale, prompts, groups, lengths_ref, chosen_ref, shares_ref, q_ref, k_ref, v_ref, slot_ref, share_ref, out_ref, line_ref
):
    rows, top = chosen_ref.shape
    columns = slot_ref.shape[1]
    column = lax.broadcasted_iota(jnp.int32, (rows, columns), 1)
    expert, place = column // SLOTS, column % SLOTS
    chosen, shares = chosen_ref[...], shares_ref[...]
    named = jnp.zeros((rows, columns), F32)
    share = jnp.zeros((rows, columns), F32)
    for k in range(top):
        hit = chosen[:, k : k + 1] == expert
        named = jnp.where(hit, 1.0, named)
        share = jnp.where(hit, shares[:, k : k + 1], share)
    here = lax.broadcasted_iota(jnp.int32, (rows, rows), 0)
    there = lax.broadcasted_iota(jnp.int32, (rows, rows), 1)
    before = jnp.where(there < here, 1.0, 0.0).astype(BF16)
    earlier = jnp.dot(before, named.astype(BF16), preferred_element_type=F32)
    taken = (named > 0.5) & (earlier == place.astype(F32))
    own = rows // prompts
    turn = jnp.where(there == (here % own) * prompts + here // own, 1.0, 0.0).astype(BF16)

    def turned(value):
        return jnp.dot(turn, value, preferred_element_type=F32).astype(BF16)

    share = jnp.where(taken, share, 0.0)
    high = share.astype(BF16)
    low = (share - high.astype(F32)).astype(BF16)
    slot_ref[...] = turned(jnp.where(taken, 1.0, 0.0).astype(BF16))
    share_ref[:rows] = turned(high)
    share_ref[rows:] = turned(low)

    count, width = q_ref.shape
    samples = lengths_ref.shape[0]
    trailing = k_ref.shape[0]
    per_sample, per_group = count // samples, count // samples // groups
    longest = trailing // samples // groups
    row = lax.broadcasted_iota(jnp.int32, (count, trailing), 0)
    col = lax.broadcasted_iota(jnp.int32, (count, trailing), 1)
    sample = row // per_sample
    length = jnp.zeros((count, trailing), jnp.int32)
    for b in range(samples):
        length = jnp.where(sample == b, lengths_ref[b], length)
    live = (
        (sample == col // (longest * groups))
        & (row // per_group % groups == col % groups)
        & (col // groups % longest < length)
    )
    scores = lax.dot_general(q_ref[...], k_ref[...], (((1,), (1,)), ((), ())), preferred_element_type=F32) * scale
    scores = jnp.where(live, scores, -1e30)
    peak = jnp.max(scores, axis=1, keepdims=True)
    terms = jnp.where(live, jnp.exp(scores - peak), 0.0)
    total = jnp.sum(terms, axis=1, keepdims=True)
    out_ref[...] = jnp.dot(terms.astype(BF16), v_ref[...], preferred_element_type=F32) / total
    line_ref[...] = jnp.transpose(jnp.broadcast_to(peak + jnp.log(total), (count, width)))[0:1, :]


def local_work(scale, prompts, experts, lengths, routed_experts, routing_weights, queries, keys, values):
    own, heads, width = queries.shape
    groups = keys.shape[2]
    top = routed_experts.shape[2]
    rows = own * prompts
    vmem = pl.BlockSpec(memory_space=pltpu.VMEM)
    return pl.pallas_call(
        functools.partial(local_kernel, scale, prompts, groups),
        in_specs=[pl.BlockSpec(memory_space=pltpu.SMEM)] + [vmem] * 5,
        out_specs=[vmem] * 4,
        out_shape=[
            jax.ShapeDtypeStruct((rows, experts * SLOTS), BF16),
            jax.ShapeDtypeStruct((2 * rows, experts * SLOTS), BF16),
            jax.ShapeDtypeStruct((own * heads, width), F32),
            jax.ShapeDtypeStruct((1, own * heads), F32),
        ],
        cost_estimate=pl.CostEstimate(flops=10**7, bytes_accessed=10**6, transcendentals=10**5),
        name="local_work",
    )(
        lengths,
        routed_experts.reshape(rows, top),
        routing_weights.reshape(rows, top),
        queries.reshape(own * heads, width),
        keys.reshape(-1, width),
        values.reshape(-1, width),
    )


def columns_kernel(in_ref, out_ref):
    parts, _, width = out_ref.shape
    for part in range(parts):
        out_ref[part] = in_ref[:, part * width : (part + 1) * width]


def columns_first(array, parts):
    rows, width = array.shape
    vmem = pl.BlockSpec(memory_space=pltpu.VMEM)
    return pl.pallas_call(
        columns_kernel,
        in_specs=[vmem],
        out_specs=vmem,
        out_shape=jax.ShapeDtypeStruct((parts, rows, width // parts), array.dtype),
        cost_estimate=pl.CostEstimate(flops=0, bytes_accessed=4 * array.size, transcendentals=0),
        name="columns_first",
    )(array)


def swap(array, distance):
    return lax.ppermute(array, "y", [(i, i ^ distance) for i in range(lax.axis_size("y"))])


def everyone(array, axes):
    copies = jnp.broadcast_to(array[None], (lax.axis_size(axes),) + array.shape)
    return lax.all_to_all(copies, axes, split_axis=0, concat_axis=0, tiled=True)


def suffix_part(own_query, keys, values, lengths, scale):
    scores = jnp.einsum("bgqd,bjgd->bgqj", own_query, keys, preferred_element_type=F32) * scale
    live = (jnp.arange(keys.shape[1], dtype=jnp.int32)[None, :] < lengths[:, None])[:, None, None, :]
    scores = jnp.where(live, scores, -1e30)
    peak = jnp.max(scores, axis=3)
    terms = jnp.where(live, jnp.exp(scores - peak[..., None]), 0.0)
    total = jnp.sum(terms, axis=3)
    summed = jnp.einsum("bgqj,bjgd->bgqd", terms.astype(BF16), values, preferred_element_type=F32)
    return summed / total[..., None], peak + jnp.log(total)


def body(
    queries,
    prefix_keys,
    prompt_value_rows,
    generated_keys,
    generated_values,
    suffix_lengths,
    hidden_rows,
    routed_experts,
    routing_weights,
    gate_weight,
    up_weight,
    down_weight,
):
    prompts = lax.axis_size("x")
    own, heads, width = queries.shape[1:]
    scale = width ** (-0.5)

    features = hidden_rows.shape[2]
    quarter = features // prompts
    experts = lax.axis_size(("z", "y", "c")) * gate_weight.shape[0]
    kv = jnp.stack([prefix_keys[0].transpose(1, 0, 2), prompt_value_rows[0].transpose(1, 0, 2)])
    kv, hidden_rows = lax.optimization_barrier((kv, hidden_rows))
    own_columns = columns_first(hidden_rows[0], prompts)
    kv_all = lax.all_gather(kv, ("z", "c"), axis=0, tiled=False)
    q_pair = jnp.concatenate([queries, swap(queries, NEAR)])

    row_quarter = lax.all_to_all(own_columns, "x", split_axis=0, concat_axis=0, tiled=True)
    slot, share, suffix_out, suffix_line = local_work(
        scale,
        prompts,
        experts,
        suffix_lengths[0],
        routed_experts,
        routing_weights,
        queries[0],
        generated_keys[0],
        generated_values[0],
    )
    row_quarter, q_pair, slot, share, suffix_out, suffix_line = lax.optimization_barrier(
        (row_quarter, q_pair, slot, share, suffix_out, suffix_line)
    )
    sent = jnp.einsum(
        "rc,rd->cd", slot, row_quarter.reshape(prompts * own, quarter), preferred_element_type=F32
    ).astype(BF16)
    arrived = lax.all_to_all(sent.reshape(experts, SLOTS, quarter), ("z", "y", "c"), split_axis=0, concat_axis=0, tiled=True)
    q_parts = [q_pair] + [swap(q_pair, i) for i in range(1, NEAR)]
    arrived, q_parts = lax.optimization_barrier((arrived, q_parts))
    pieces = everyone(arrived.reshape(experts * SLOTS, quarter), "x")
    sums = attention(q_parts, kv_all, scale)
    pieces, sums = lax.optimization_barrier((pieces, sums))
    parts = lax.all_to_all(
        expert_parts(pieces, gate_weight[0], up_weight[0], down_weight[0]), "x", split_axis=0, concat_axis=0, tiled=True
    )
    sums = [sums[0]] + [swap(sums[i], i) for i in range(1, NEAR)]
    parts, sums = lax.optimization_barrier((parts, sums))
    expert_sum = jnp.sum(parts.astype(F32), axis=0).astype(BF16)
    returned = lax.all_to_all(
        expert_sum.reshape(experts, SLOTS, quarter), ("z", "y", "c"), split_axis=0, concat_axis=0, tiled=True
    ).reshape(experts * SLOTS, quarter)
    mine, send = merge(sums)
    other = swap(send, NEAR)
    returned, mine, other = lax.optimization_barrier((returned, mine, other))
    mixed = jnp.dot(share, returned, preferred_element_type=F32)
    mixed = (mixed[: prompts * own] + mixed[prompts * own :]).astype(BF16).reshape(prompts, own, quarter)
    mixed = lax.all_to_all(mixed, "x", split_axis=0, concat_axis=0, tiled=True)
    expert_mix = jnp.concatenate([mixed[p] for p in range(prompts)], axis=1)[None]

    attended = last_merge(mine, other, suffix_out, suffix_line).reshape(1, own, heads, width)
    return attended, expert_mix


def solution(mesh):
    prompts = mesh.shape["prompt"]
    ctx = mesh.shape["ctx"]
    across = math.isqrt(ctx // 2)
    grid = Mesh(mesh.devices.reshape(prompts, across, across, 2), ("x", "z", "y", "c"))
    lay = ("z", "y", "c")
    placed = (
        P("x", lay, None, None),
        P("x", lay, None, None),
        P("x", lay, None, None),
        P("x", lay, None, None, None),
        P("x", lay, None, None, None),
        P("x", lay),
        P("x", lay, None),
        P(lay, None, None),
        P(lay, None, None),
        P(lay, "x", None),
        P(lay, "x", None),
        P(lay, "x", None),
    )
    return jax.shard_map(
        body,
        mesh=grid,
        in_specs=placed,
        out_specs=(P("x", lay, None, None), P("x", lay, None)),
        check_vma=False,
    )
```

```python
import functools
import math

import jax
import jax.numpy as jnp
from jax import lax
from jax.experimental import pallas as pl
from jax.experimental.pallas import tpu as pltpu
from jax.sharding import Mesh
from jax.sharding import PartitionSpec as P

BF16 = jnp.bfloat16
F32 = jnp.float32
LOG2E = 1.4426950408889634
NEAR = 4
SLOTS = 2
LANES = 128
EXTRA = 16


def three_parts(value):
    high = value.astype(BF16)
    rest = value - high.astype(F32)
    middle = rest.astype(BF16)
    low = (rest - middle.astype(F32)).astype(BF16)
    return high, middle, low


def pack(out_ref, at, values, line):
    rows, width = values.shape
    parts = [part.astype(F32) for part in three_parts(line)]
    extra = jnp.concatenate(parts + [jnp.zeros((EXTRA - 3, width), F32)], axis=0).astype(BF16)
    at = at if isinstance(at, tuple) else (at,)
    out_ref[at + (slice(0, rows),)] = values.astype(BF16)
    out_ref[at + (slice(rows, rows + EXTRA),)] = extra


def unpack_line(ref, at, rows):
    logs = ref[at, rows:, :].astype(F32)
    return logs[0:1] + logs[1:2] + logs[2:3]


def attention_kernel(scale, *refs):
    q_refs, kv_ref, out_ref = refs[:NEAR], refs[NEAR], refs[NEAR + 1]
    q_buf, k_buf, v_buf, vaug, out_buf, q_sem, kv_sem, out_sem = refs[NEAR + 2 :]
    samples, groups, per_group, width = q_refs[0].shape
    dests = out_ref.shape[0] // NEAR
    own = samples // dests
    positions = kv_ref.shape[0] * kv_ref.shape[3]
    q_in = [pltpu.make_async_copy(q_refs[i], q_buf.at[i], q_sem.at[i]) for i in range(NEAR)]
    kv_in = [
        [pltpu.make_async_copy(kv_ref.at[:, i, g], buf.at[g], kv_sem.at[i, g]) for i, buf in enumerate((k_buf, v_buf))]
        for g in range(groups)
    ]
    for copy in q_in + kv_in[0] + kv_in[1]:
        copy.start()
    for g in range(groups):
        vaug[g, :, width:] = jnp.ones((positions, width), BF16)
    for copy in q_in + kv_in[0] + kv_in[1]:
        copy.wait()
    outs, logs = {}, {}
    for g in range(groups):
        vaug[g, :, :width] = v_buf[g].reshape(positions, width)
    for g in range(groups):
        keys = k_buf[g].reshape(positions, width)
        for first in (0, 2):
            rows = jnp.concatenate(
                [q_buf[first + i, :, g].reshape(samples * per_group, width) for i in range(2)], axis=0
            )
            scores = lax.dot_general(rows, keys, (((1,), (1,)), ((), ())), preferred_element_type=F32)
            peak = jnp.max(scores, axis=1, keepdims=True)
            probs = jnp.exp2((scores - peak) * (scale * LOG2E)).astype(BF16)
            summed = jnp.dot(probs, vaug[g], preferred_element_type=F32)
            total = summed[:, width:]
            outs[g, first] = (summed[:, :width] / total).reshape(2 * samples, 1, per_group, width)
            logs[g, first] = (peak * scale + jnp.log(total)).reshape(2 * samples, 1, per_group, width)
    shape = (2 * dests, own * groups * per_group, width)
    for first in (0, 2):
        values = jnp.concatenate([outs[g, first] for g in range(groups)], axis=1).reshape(shape)
        joined = jnp.concatenate([logs[g, first] for g in range(groups)], axis=1).reshape(shape)
        for i in range(2):
            for d in range(dests):
                at = i * dests + d
                pack(out_buf, first + i + NEAR * d, values[at], jnp.transpose(joined[at])[0:1, :])
    out = pltpu.make_async_copy(out_buf, out_ref, out_sem)
    out.start()
    out.wait()


def attention(q_parts, kv_all, scale):
    sources, own, heads, width = q_parts[0].shape
    groups = kv_all.shape[2]
    samples = sources * own
    positions = kv_all.shape[0] * kv_all.shape[3]
    pairs = NEAR * samples * heads * positions
    views = [q.reshape(samples, groups, heads // groups, width) for q in q_parts]
    sums = jax.ShapeDtypeStruct((NEAR * sources, own * heads + EXTRA, width), BF16)
    hbm = pl.BlockSpec(memory_space=pltpu.HBM)
    gathered = (groups, kv_all.shape[0], kv_all.shape[3], width)
    return pl.pallas_call(
        lambda *refs: attention_kernel(scale, *refs),
        in_specs=[hbm] * (NEAR + 1),
        out_specs=hbm,
        out_shape=sums,
        scratch_shapes=[
            pltpu.VMEM((NEAR,) + views[0].shape, BF16),
            pltpu.VMEM(gathered, BF16),
            pltpu.VMEM(gathered, BF16),
            pltpu.VMEM((groups, positions, 2 * width), BF16),
            pltpu.VMEM(sums.shape, BF16),
            pltpu.SemaphoreType.DMA((NEAR,)),
            pltpu.SemaphoreType.DMA((2, groups)),
            pltpu.SemaphoreType.DMA,
        ],
        compiler_params=pltpu.CompilerParams(vmem_limit_bytes=60 * 1024 * 1024),
        cost_estimate=pl.CostEstimate(
            flops=6 * pairs * width, bytes_accessed=2 * (kv_all.size + 8 * q_parts[0].size), transcendentals=pairs
        ),
        name="prompt_attention",
    )(*views, kv_all)


def merged(values, lines):
    highest = functools.reduce(jnp.maximum, lines)
    weights = [jnp.exp(line - highest) for line in lines]
    total = sum(weights)
    shape = values[0].shape
    result = sum(v * jnp.transpose(jnp.broadcast_to(w / total, shape)) for v, w in zip(values, weights, strict=True))
    return result, highest + jnp.log(total)


def merge_kernel(place_ref, all_ref, suffix_ref, suffix_log_ref, out_ref, buf, sems):
    rows = out_ref.shape[0]
    sources = all_ref.shape[0]
    copies = [
        pltpu.make_async_copy(all_ref.at[i, place_ref[0] ^ i], buf.at[i], sems.at[i]) for i in range(sources)
    ]
    for copy in copies:
        copy.start()
    for copy in copies:
        copy.wait()
    values, _ = merged(
        [buf[i, :rows, :].astype(F32) for i in range(sources)] + [suffix_ref[...]],
        [unpack_line(buf, i, rows) for i in range(sources)] + [suffix_log_ref[...]],
    )
    out_ref[...] = values.astype(BF16)


def merge(place, gathered, suffix, suffix_log):
    vmem = pl.BlockSpec(memory_space=pltpu.VMEM)
    return pl.pallas_call(
        merge_kernel,
        in_specs=[pl.BlockSpec(memory_space=pltpu.SMEM), pl.BlockSpec(memory_space=pltpu.HBM), vmem, vmem],
        out_specs=vmem,
        out_shape=jax.ShapeDtypeStruct(suffix.shape, BF16),
        scratch_shapes=[
            pltpu.VMEM((gathered.shape[0],) + gathered.shape[2:], BF16),
            pltpu.SemaphoreType.DMA((gathered.shape[0],)),
        ],
        compiler_params=pltpu.CompilerParams(vmem_limit_bytes=62 * 1024 * 1024),
        cost_estimate=pl.CostEstimate(flops=60 * suffix.size, bytes_accessed=30 * suffix.size, transcendentals=0),
        name="merge_partials",
    )(place, gathered, suffix, suffix_log)


def act_kernel(rows_ref, gate_ref, up_ref, out_ref):
    parts, rows, width = rows_ref.shape
    dims = (((1,), (1,)), ((), ()))
    gate = up = None
    for part in range(parts):
        columns = slice(part * width, (part + 1) * width)
        piece = rows_ref[part]
        more_gate = lax.dot_general(piece, gate_ref[:, columns], dims, preferred_element_type=F32)
        more_up = lax.dot_general(piece, up_ref[:, columns], dims, preferred_element_type=F32)
        gate = more_gate if gate is None else gate + more_gate
        up = more_up if up is None else up + more_up
    act = gate / (1.0 + jnp.exp(-gate)) * up
    half, lanes = rows // 2, out_ref.shape[2]
    head = act[:, :lanes].astype(BF16)
    tail = jnp.concatenate([act[:half, lanes:], act[half:, lanes:]], axis=1).astype(BF16)
    for part in range(parts):
        out_ref[part, :rows, :] = head
        out_ref[part, rows:, :] = tail


def expert_act(pieces, gate_weight, up_weight):
    parts, rows, width = pieces.shape
    units = gate_weight.shape[0]
    vmem = pl.BlockSpec(memory_space=pltpu.VMEM)
    return pl.pallas_call(
        act_kernel,
        in_specs=[vmem] * 3,
        out_specs=vmem,
        out_shape=jax.ShapeDtypeStruct((parts, rows * units // LANES, LANES), BF16),
        compiler_params=pltpu.CompilerParams(vmem_limit_bytes=24 * 1024 * 1024),
        cost_estimate=pl.CostEstimate(
            flops=4 * rows * width * parts * units,
            bytes_accessed=4 * gate_weight.size + 2 * pieces.size,
            transcendentals=rows * units,
        ),
        name="expert_act",
    )(pieces, gate_weight, up_weight)


def out_kernel(units, act_ref, down_ref, out_ref):
    rows, _ = out_ref.shape
    half, rest = rows // 2, units - LANES
    total = None
    for part in range(act_ref.shape[0]):
        tail = act_ref[part, rows:, :]
        weight = down_ref[part, LANES:units, :]
        more = jnp.dot(act_ref[part, :rows, :], down_ref[part, :LANES, :], preferred_element_type=F32)
        more = more + jnp.concatenate(
            [
                jnp.dot(tail[:, :rest], weight, preferred_element_type=F32),
                jnp.dot(tail[:, rest:], weight, preferred_element_type=F32),
            ],
            axis=0,
        )
        total = more if total is None else total + more
    out_ref[...] = total.astype(BF16)


def expert_out(acts, downs, units):
    parts, _, width = downs.shape
    rows = acts.shape[1] * LANES // units
    vmem = pl.BlockSpec(memory_space=pltpu.VMEM)
    return pl.pallas_call(
        functools.partial(out_kernel, units),
        in_specs=[vmem] * 2,
        out_specs=vmem,
        out_shape=jax.ShapeDtypeStruct((rows, width), BF16),
        compiler_params=pltpu.CompilerParams(vmem_limit_bytes=24 * 1024 * 1024),
        cost_estimate=pl.CostEstimate(
            flops=2 * rows * width * parts * units,
            bytes_accessed=2 * (downs.size + acts.size),
            transcendentals=0,
        ),
        name="expert_out",
    )(acts, downs)


def local_kernel(
    scale, prompts, groups, lengths_ref, chosen_ref, shares_ref, q_ref, k_ref, v_ref, slot_ref, share_ref, out_ref, line_ref
):
    rows, top = chosen_ref.shape
    columns = slot_ref.shape[1]
    column = lax.broadcasted_iota(jnp.int32, (rows, columns), 1)
    expert, place = column // SLOTS, column % SLOTS
    chosen, shares = chosen_ref[...], shares_ref[...]
    named = jnp.zeros((rows, columns), F32)
    share = jnp.zeros((rows, columns), F32)
    for k in range(top):
        hit = chosen[:, k : k + 1] == expert
        named = jnp.where(hit, 1.0, named)
        share = jnp.where(hit, shares[:, k : k + 1], share)
    here = lax.broadcasted_iota(jnp.int32, (rows, rows), 0)
    there = lax.broadcasted_iota(jnp.int32, (rows, rows), 1)
    before = jnp.where(there < here, 1.0, 0.0).astype(BF16)
    earlier = jnp.dot(before, named.astype(BF16), preferred_element_type=F32)
    taken = (named > 0.5) & (earlier == place.astype(F32))
    own = rows // prompts
    turn = jnp.where(there == (here % own) * prompts + here // own, 1.0, 0.0).astype(BF16)

    def turned(value):
        return jnp.dot(turn, value, preferred_element_type=F32).astype(BF16)

    share = jnp.where(taken, share, 0.0)
    high = share.astype(BF16)
    low = (share - high.astype(F32)).astype(BF16)
    slot_ref[...] = turned(jnp.where(taken, 1.0, 0.0).astype(BF16))
    share_ref[:rows] = turned(high)
    share_ref[rows:] = turned(low)

    count, width = q_ref.shape
    samples = lengths_ref.shape[0]
    trailing = k_ref.shape[0]
    per_sample, per_group = count // samples, count // samples // groups
    longest = trailing // samples // groups
    row = lax.broadcasted_iota(jnp.int32, (count, trailing), 0)
    col = lax.broadcasted_iota(jnp.int32, (count, trailing), 1)
    sample = row // per_sample
    length = jnp.zeros((count, trailing), jnp.int32)
    for b in range(samples):
        length = jnp.where(sample == b, lengths_ref[b], length)
    live = (
        (sample == col // (longest * groups))
        & (row // per_group % groups == col % groups)
        & (col // groups % longest < length)
    )
    scores = lax.dot_general(q_ref[...], k_ref[...], (((1,), (1,)), ((), ())), preferred_element_type=F32) * scale
    scores = jnp.where(live, scores, -1e30)
    peak = jnp.max(scores, axis=1, keepdims=True)
    terms = jnp.where(live, jnp.exp(scores - peak), 0.0)
    total = jnp.sum(terms, axis=1, keepdims=True)
    out_ref[...] = jnp.dot(terms.astype(BF16), v_ref[...], preferred_element_type=F32) / total
    line_ref[...] = jnp.transpose(jnp.broadcast_to(peak + jnp.log(total), (count, width)))[0:1, :]


def local_work(scale, prompts, experts, lengths, routed_experts, routing_weights, queries, keys, values):
    own, heads, width = queries.shape
    groups = keys.shape[2]
    top = routed_experts.shape[2]
    rows = own * prompts
    vmem = pl.BlockSpec(memory_space=pltpu.VMEM)
    return pl.pallas_call(
        functools.partial(local_kernel, scale, prompts, groups),
        in_specs=[pl.BlockSpec(memory_space=pltpu.SMEM)] + [vmem] * 5,
        out_specs=[vmem] * 4,
        out_shape=[
            jax.ShapeDtypeStruct((rows, experts * SLOTS), BF16),
            jax.ShapeDtypeStruct((2 * rows, experts * SLOTS), BF16),
            jax.ShapeDtypeStruct((own * heads, width), F32),
            jax.ShapeDtypeStruct((1, own * heads), F32),
        ],
        cost_estimate=pl.CostEstimate(flops=10**7, bytes_accessed=10**6, transcendentals=10**5),
        name="local_work",
    )(
        lengths,
        routed_experts.reshape(rows, top),
        routing_weights.reshape(rows, top),
        queries.reshape(own * heads, width),
        keys.reshape(-1, width),
        values.reshape(-1, width),
    )


def columns_kernel(down_ref, rows_ref, out_ref):
    units, own = down_ref.shape[0], rows_ref.shape[0]
    parts, lines, width = out_ref.shape
    for part in range(parts):
        columns = slice(part * width, (part + 1) * width)
        out_ref[part, :units, :] = down_ref[:, columns]
        rows = rows_ref[:, columns].astype(F32)
        blank = jnp.zeros((lines - units - own, width), F32)
        out_ref[part, units:, :] = jnp.concatenate([rows, blank], axis=0).astype(BF16)


def columns_first(down_weight, rows, parts):
    units, features = down_weight.shape
    vmem = pl.BlockSpec(memory_space=pltpu.VMEM)
    return pl.pallas_call(
        columns_kernel,
        in_specs=[vmem] * 2,
        out_specs=vmem,
        out_shape=jax.ShapeDtypeStruct((parts, units + 8, features // parts), BF16),
        cost_estimate=pl.CostEstimate(flops=0, bytes_accessed=4 * down_weight.size, transcendentals=0),
        name="columns_first",
    )(down_weight, rows)


def swap(array, distance):
    return lax.ppermute(array, "y", [(i, i ^ distance) for i in range(lax.axis_size("y"))])


def exchange(array, axes):
    return lax.all_to_all(array, axes, split_axis=0, concat_axis=0, tiled=True)


def body(
    queries,
    prefix_keys,
    prompt_value_rows,
    generated_keys,
    generated_values,
    suffix_lengths,
    hidden_rows,
    routed_experts,
    routing_weights,
    gate_weight,
    up_weight,
    down_weight,
):
    prompts = lax.axis_size("x")
    own, heads, width = queries.shape[1:]
    scale = width ** (-0.5)

    features = hidden_rows.shape[2]
    quarter = features // prompts
    experts = lax.axis_size(("z", "y", "c")) * gate_weight.shape[0]
    kv = jnp.stack([prefix_keys[0].transpose(1, 0, 2), prompt_value_rows[0].transpose(1, 0, 2)])
    kv, hidden_rows = lax.optimization_barrier((kv, hidden_rows))
    own_columns = columns_first(down_weight[0], hidden_rows[0], prompts)
    kv_all = lax.all_gather(kv, ("z", "c"), axis=0, tiled=False)
    q_pair = jnp.concatenate([queries, swap(queries, NEAR)])

    units = down_weight.shape[1]
    downs = exchange(own_columns, "x")
    row_quarter = downs[:, units : units + own]
    slot, share, suffix_out, suffix_line = local_work(
        scale,
        prompts,
        experts,
        suffix_lengths[0],
        routed_experts,
        routing_weights,
        queries[0],
        generated_keys[0],
        generated_values[0],
    )
    row_quarter, q_pair, slot, share, suffix_out, suffix_line = lax.optimization_barrier(
        (row_quarter, q_pair, slot, share, suffix_out, suffix_line)
    )
    sent = jnp.einsum(
        "rc,rd->cd", slot, row_quarter.reshape(prompts * own, quarter), preferred_element_type=F32
    ).astype(BF16)
    arrived = lax.all_to_all(sent.reshape(experts, SLOTS, quarter), ("z", "y", "c"), split_axis=0, concat_axis=0, tiled=True)
    q_parts = [q_pair] + [swap(q_pair, i) for i in range(1, NEAR)]
    arrived, q_parts = lax.optimization_barrier((arrived, q_parts))
    pieces = arrived.reshape(experts * SLOTS, quarter)
    pieces = exchange(jnp.broadcast_to(pieces[None], (prompts,) + pieces.shape), "x")
    sums = attention(q_parts, kv_all, scale)
    pieces, sums = lax.optimization_barrier((pieces, sums))
    gathered = lax.all_gather(sums, "y", axis=0, tiled=False)
    acts = exchange(expert_act(pieces, gate_weight[0], up_weight[0]), "x")
    outcome = expert_out(acts, downs, units).reshape(experts, SLOTS, quarter)
    returned = exchange(outcome, ("z", "y", "c")).reshape(experts * SLOTS, quarter)
    mixed = jnp.dot(share, returned, preferred_element_type=F32)
    mixed = (mixed[: prompts * own] + mixed[prompts * own :]).astype(BF16).reshape(prompts, own, quarter)
    mixed = exchange(mixed, "x")
    place = lax.axis_index("y").astype(jnp.int32).reshape(1)
    attended = merge(place, gathered, suffix_out, suffix_line)
    mixed, attended = lax.optimization_barrier((mixed, attended))
    expert_mix = jnp.concatenate([mixed[p] for p in range(prompts)], axis=1)[None]
    attended = attended.reshape(1, own, heads, width)
    return attended, expert_mix


def solution(mesh):
    prompts = mesh.shape["prompt"]
    ctx = mesh.shape["ctx"]
    across = math.isqrt(ctx // 2)
    grid = Mesh(mesh.devices.reshape(prompts, across, across, 2), ("x", "z", "y", "c"))
    lay = ("z", "y", "c")
    placed = (
        P("x", lay, None, None),
        P("x", lay, None, None),
        P("x", lay, None, None),
        P("x", lay, None, None, None),
        P("x", lay, None, None, None),
        P("x", lay),
        P("x", lay, None),
        P(lay, None, None),
        P(lay, None, None),
        P(lay, "x", None),
        P(lay, "x", None),
        P(lay, "x", None),
    )
    return jax.shard_map(
        body,
        mesh=grid,
        in_specs=placed,
        out_specs=(P("x", lay, None, None), P("x", lay, None)),
        check_vma=False,
    )
```

```python
import functools
import math

import jax
import jax.numpy as jnp
from jax import lax
from jax.experimental import pallas as pl
from jax.experimental.pallas import tpu as pltpu
from jax.sharding import Mesh
from jax.sharding import PartitionSpec as P

BF16 = jnp.bfloat16
F32 = jnp.float32
LOG2E = 1.4426950408889634
NEAR = 4
SLOTS = 2
LANES = 128
TERMS = 3


def three_parts(value):
    high = value.astype(BF16)
    rest = value - high.astype(F32)
    middle = rest.astype(BF16)
    low = (rest - middle.astype(F32)).astype(BF16)
    return high, middle, low


def attention_kernel(scale, *refs):
    q_refs, kv_ref, out_ref = refs[:NEAR], refs[NEAR], refs[NEAR + 1]
    q_buf, k_buf, v_buf, vaug, out_buf, q_sem, kv_sem, out_sem = refs[NEAR + 2 :]
    samples, groups, per_group, width = q_refs[0].shape
    own = samples * groups * per_group // width
    dests, own = own, samples // own
    positions = kv_ref.shape[0] * kv_ref.shape[3]
    q_in = [pltpu.make_async_copy(q_refs[i], q_buf.at[i], q_sem.at[i]) for i in range(NEAR)]
    kv_in = [
        [pltpu.make_async_copy(kv_ref.at[:, i, g], buf.at[g], kv_sem.at[i, g]) for i, buf in enumerate((k_buf, v_buf))]
        for g in range(groups)
    ]
    for copy in q_in + kv_in[0] + kv_in[1]:
        copy.start()
    for g in range(groups):
        vaug[g, :, width:] = jnp.ones((positions, width), BF16)
    for copy in q_in + kv_in[0] + kv_in[1]:
        copy.wait()
    outs, logs, lines = {}, {}, {}
    for g in range(groups):
        vaug[g, :, :width] = v_buf[g].reshape(positions, width)
    for g in range(groups):
        keys = k_buf[g].reshape(positions, width)
        for first in (0, 2):
            rows = jnp.concatenate(
                [q_buf[first + i, :, g].reshape(samples * per_group, width) for i in range(2)], axis=0
            )
            scores = lax.dot_general(rows, keys, (((1,), (1,)), ((), ())), preferred_element_type=F32)
            peak = jnp.max(scores, axis=1, keepdims=True)
            probs = jnp.exp2((scores - peak) * (scale * LOG2E)).astype(BF16)
            summed = jnp.dot(probs, vaug[g], preferred_element_type=F32)
            total = summed[:, width:]
            outs[g, first] = (summed[:, :width] / total).reshape(2 * samples, 1, per_group, width)
            logs[g, first] = (peak * scale + jnp.log(total)).reshape(2 * samples, 1, per_group, width)
    shape = (2 * dests, own * groups * per_group, width)
    for first in (0, 2):
        values = jnp.concatenate([outs[g, first] for g in range(groups)], axis=1).reshape(shape)
        joined = jnp.concatenate([logs[g, first] for g in range(groups)], axis=1).reshape(shape)
        for i in range(2):
            for d in range(dests):
                at = i * dests + d
                to = first + i + NEAR * d
                out_buf[to * width : (to + 1) * width, :] = values[at].astype(BF16)
                lines[to] = [part.astype(F32) for part in three_parts(jnp.transpose(joined[at])[0:1, :])]
    used = NEAR * dests * width
    extra = sum([lines[to] for to in range(NEAR * dests)], [])
    extra.append(jnp.zeros((out_ref.shape[0] - used - len(extra), width), F32))
    out_buf[used:, :] = jnp.concatenate(extra, axis=0).astype(BF16)
    out = pltpu.make_async_copy(out_buf, out_ref, out_sem)
    out.start()
    out.wait()


def attention(q_parts, kv_all, scale):
    sources, own, heads, width = q_parts[0].shape
    groups = kv_all.shape[2]
    samples = sources * own
    positions = kv_all.shape[0] * kv_all.shape[3]
    pairs = NEAR * samples * heads * positions
    views = [q.reshape(samples, groups, heads // groups, width) for q in q_parts]
    count = NEAR * sources
    sums = jax.ShapeDtypeStruct((count * own * heads + -(-count * TERMS // 16) * 16, width), BF16)
    hbm = pl.BlockSpec(memory_space=pltpu.HBM)
    gathered = (groups, kv_all.shape[0], kv_all.shape[3], width)
    return pl.pallas_call(
        lambda *refs: attention_kernel(scale, *refs),
        in_specs=[hbm] * (NEAR + 1),
        out_specs=hbm,
        out_shape=sums,
        scratch_shapes=[
            pltpu.VMEM((NEAR,) + views[0].shape, BF16),
            pltpu.VMEM(gathered, BF16),
            pltpu.VMEM(gathered, BF16),
            pltpu.VMEM((groups, positions, 2 * width), BF16),
            pltpu.VMEM(sums.shape, BF16),
            pltpu.SemaphoreType.DMA((NEAR,)),
            pltpu.SemaphoreType.DMA((2, groups)),
            pltpu.SemaphoreType.DMA,
        ],
        compiler_params=pltpu.CompilerParams(vmem_limit_bytes=60 * 1024 * 1024),
        cost_estimate=pl.CostEstimate(
            flops=6 * pairs * width, bytes_accessed=2 * (kv_all.size + 8 * q_parts[0].size), transcendentals=pairs
        ),
        name="prompt_attention",
    )(*views, kv_all)


def merged(values, lines):
    highest = functools.reduce(jnp.maximum, lines)
    weights = [jnp.exp(line - highest) for line in lines]
    total = sum(weights)
    shape = values[0].shape
    result = sum(v * jnp.transpose(jnp.broadcast_to(w / total, shape)) for v, w in zip(values, weights, strict=True))
    return result, highest + jnp.log(total)


def merge_kernel(place_ref, all_ref, suffix_ref, suffix_log_ref, out_ref, buf, extra, sems):
    rows = out_ref.shape[0]
    sources, lines = extra.shape[:2]
    copies = []
    for i in range(sources):
        start = pl.multiple_of((place_ref[0] ^ i) * rows, rows)
        copies.append(pltpu.make_async_copy(all_ref.at[i, pl.ds(start, rows)], buf.at[i], sems.at[0, i]))
        copies.append(
            pltpu.make_async_copy(all_ref.at[i, pl.ds(sources * rows, lines)], extra.at[i], sems.at[1, i])
        )
    for copy in copies:
        copy.start()
    for copy in copies:
        copy.wait()
    owner = lax.broadcasted_iota(jnp.int32, extra.shape[1:], 0) // TERMS
    logs = [
        jnp.sum(jnp.where(owner == (place_ref[0] ^ i), extra[i].astype(F32), 0.0), axis=0, keepdims=True)
        for i in range(sources)
    ]
    values, _ = merged(
        [buf[i].astype(F32) for i in range(sources)] + [suffix_ref[...]], logs + [suffix_log_ref[...]]
    )
    out_ref[...] = values.astype(BF16)


def merge(place, gathered, suffix, suffix_log):
    sources, lines, width = gathered.shape
    rows = suffix.shape[0]
    vmem = pl.BlockSpec(memory_space=pltpu.VMEM)
    return pl.pallas_call(
        merge_kernel,
        in_specs=[pl.BlockSpec(memory_space=pltpu.SMEM), pl.BlockSpec(memory_space=pltpu.HBM), vmem, vmem],
        out_specs=vmem,
        out_shape=jax.ShapeDtypeStruct(suffix.shape, BF16),
        scratch_shapes=[
            pltpu.VMEM((sources, rows, width), BF16),
            pltpu.VMEM((sources, lines - sources * rows, width), BF16),
            pltpu.SemaphoreType.DMA((2, sources)),
        ],
        compiler_params=pltpu.CompilerParams(vmem_limit_bytes=62 * 1024 * 1024),
        cost_estimate=pl.CostEstimate(flops=60 * suffix.size, bytes_accessed=30 * suffix.size, transcendentals=0),
        name="merge_partials",
    )(place, gathered, suffix, suffix_log)


def act_kernel(rows_ref, gate_ref, up_ref, out_ref):
    parts, rows, width = rows_ref.shape
    dims = (((1,), (1,)), ((), ()))
    gate = up = None
    for part in range(parts):
        columns = slice(part * width, (part + 1) * width)
        piece = rows_ref[part]
        more_gate = lax.dot_general(piece, gate_ref[:, columns], dims, preferred_element_type=F32)
        more_up = lax.dot_general(piece, up_ref[:, columns], dims, preferred_element_type=F32)
        gate = more_gate if gate is None else gate + more_gate
        up = more_up if up is None else up + more_up
    act = gate / (1.0 + jnp.exp(-gate)) * up
    half, lanes = rows // 2, out_ref.shape[2]
    head = act[:, :lanes].astype(BF16)
    tail = jnp.concatenate([act[:half, lanes:], act[half:, lanes:]], axis=1).astype(BF16)
    for part in range(parts):
        out_ref[part, :rows, :] = head
        out_ref[part, rows:, :] = tail


def expert_act(pieces, gate_weight, up_weight):
    parts, rows, width = pieces.shape
    units = gate_weight.shape[0]
    vmem = pl.BlockSpec(memory_space=pltpu.VMEM)
    return pl.pallas_call(
        act_kernel,
        in_specs=[vmem] * 3,
        out_specs=vmem,
        out_shape=jax.ShapeDtypeStruct((parts, rows * units // LANES, LANES), BF16),
        compiler_params=pltpu.CompilerParams(vmem_limit_bytes=24 * 1024 * 1024),
        cost_estimate=pl.CostEstimate(
            flops=4 * rows * width * parts * units,
            bytes_accessed=4 * gate_weight.size + 2 * pieces.size,
            transcendentals=rows * units,
        ),
        name="expert_act",
    )(pieces, gate_weight, up_weight)


def out_kernel(units, act_ref, down_ref, out_ref):
    rows, _ = out_ref.shape
    half, rest = rows // 2, units - LANES
    total = None
    for part in range(act_ref.shape[0]):
        tail = act_ref[part, rows:, :]
        weight = down_ref[part, LANES:units, :]
        more = jnp.dot(act_ref[part, :rows, :], down_ref[part, :LANES, :], preferred_element_type=F32)
        more = more + jnp.concatenate(
            [
                jnp.dot(tail[:, :rest], weight, preferred_element_type=F32),
                jnp.dot(tail[:, rest:], weight, preferred_element_type=F32),
            ],
            axis=0,
        )
        total = more if total is None else total + more
    out_ref[...] = total.astype(BF16)


def expert_out(acts, downs, units):
    parts, _, width = downs.shape
    rows = acts.shape[1] * LANES // units
    vmem = pl.BlockSpec(memory_space=pltpu.VMEM)
    return pl.pallas_call(
        functools.partial(out_kernel, units),
        in_specs=[vmem] * 2,
        out_specs=vmem,
        out_shape=jax.ShapeDtypeStruct((rows, width), BF16),
        compiler_params=pltpu.CompilerParams(vmem_limit_bytes=24 * 1024 * 1024),
        cost_estimate=pl.CostEstimate(
            flops=2 * rows * width * parts * units,
            bytes_accessed=2 * (downs.size + acts.size),
            transcendentals=0,
        ),
        name="expert_out",
    )(acts, downs)


def local_kernel(
    scale, prompts, groups, lengths_ref, chosen_ref, shares_ref, q_ref, k_ref, v_ref, slot_ref, share_ref, out_ref, line_ref
):
    rows, top = chosen_ref.shape
    columns = slot_ref.shape[1]
    column = lax.broadcasted_iota(jnp.int32, (rows, columns), 1)
    expert, place = column // SLOTS, column % SLOTS
    chosen, shares = chosen_ref[...], shares_ref[...]
    named = jnp.zeros((rows, columns), F32)
    share = jnp.zeros((rows, columns), F32)
    for k in range(top):
        hit = chosen[:, k : k + 1] == expert
        named = jnp.where(hit, 1.0, named)
        share = jnp.where(hit, shares[:, k : k + 1], share)
    here = lax.broadcasted_iota(jnp.int32, (rows, rows), 0)
    there = lax.broadcasted_iota(jnp.int32, (rows, rows), 1)
    before = jnp.where(there < here, 1.0, 0.0).astype(BF16)
    earlier = jnp.dot(before, named.astype(BF16), preferred_element_type=F32)
    taken = (named > 0.5) & (earlier == place.astype(F32))
    own = rows // prompts
    turn = jnp.where(there == (here % own) * prompts + here // own, 1.0, 0.0).astype(BF16)

    def turned(value):
        return jnp.dot(turn, value, preferred_element_type=F32).astype(BF16)

    share = jnp.where(taken, share, 0.0)
    high = share.astype(BF16)
    low = (share - high.astype(F32)).astype(BF16)
    slot_ref[...] = turned(jnp.where(taken, 1.0, 0.0).astype(BF16))
    share_ref[:rows] = turned(high)
    share_ref[rows:] = turned(low)

    count, width = q_ref.shape
    samples = lengths_ref.shape[0]
    trailing = k_ref.shape[0]
    per_sample, per_group = count // samples, count // samples // groups
    longest = trailing // samples // groups
    row = lax.broadcasted_iota(jnp.int32, (count, trailing), 0)
    col = lax.broadcasted_iota(jnp.int32, (count, trailing), 1)
    sample = row // per_sample
    length = jnp.zeros((count, trailing), jnp.int32)
    for b in range(samples):
        length = jnp.where(sample == b, lengths_ref[b], length)
    live = (
        (sample == col // (longest * groups))
        & (row // per_group % groups == col % groups)
        & (col // groups % longest < length)
    )
    scores = lax.dot_general(q_ref[...], k_ref[...], (((1,), (1,)), ((), ())), preferred_element_type=F32) * scale
    scores = jnp.where(live, scores, -1e30)
    peak = jnp.max(scores, axis=1, keepdims=True)
    terms = jnp.where(live, jnp.exp(scores - peak), 0.0)
    total = jnp.sum(terms, axis=1, keepdims=True)
    out_ref[...] = jnp.dot(terms.astype(BF16), v_ref[...], preferred_element_type=F32) / total
    line_ref[...] = jnp.transpose(jnp.broadcast_to(peak + jnp.log(total), (count, width)))[0:1, :]


def local_work(scale, prompts, experts, lengths, routed_experts, routing_weights, queries, keys, values):
    own, heads, width = queries.shape
    groups = keys.shape[2]
    top = routed_experts.shape[2]
    rows = own * prompts
    vmem = pl.BlockSpec(memory_space=pltpu.VMEM)
    return pl.pallas_call(
        functools.partial(local_kernel, scale, prompts, groups),
        in_specs=[pl.BlockSpec(memory_space=pltpu.SMEM)] + [vmem] * 5,
        out_specs=[vmem] * 4,
        out_shape=[
            jax.ShapeDtypeStruct((rows, experts * SLOTS), BF16),
            jax.ShapeDtypeStruct((2 * rows, experts * SLOTS), BF16),
            jax.ShapeDtypeStruct((own * heads, width), F32),
            jax.ShapeDtypeStruct((1, own * heads), F32),
        ],
        cost_estimate=pl.CostEstimate(flops=10**7, bytes_accessed=10**6, transcendentals=10**5),
        name="local_work",
    )(
        lengths,
        routed_experts.reshape(rows, top),
        routing_weights.reshape(rows, top),
        queries.reshape(own * heads, width),
        keys.reshape(-1, width),
        values.reshape(-1, width),
    )


def columns_kernel(down_ref, rows_ref, out_ref):
    units, own = down_ref.shape[0], rows_ref.shape[0]
    parts, lines, width = out_ref.shape
    for part in range(parts):
        columns = slice(part * width, (part + 1) * width)
        out_ref[part, :units, :] = down_ref[:, columns]
        rows = rows_ref[:, columns].astype(F32)
        blank = jnp.zeros((lines - units - own, width), F32)
        out_ref[part, units:, :] = jnp.concatenate([rows, blank], axis=0).astype(BF16)


def columns_first(down_weight, rows, parts):
    units, features = down_weight.shape
    vmem = pl.BlockSpec(memory_space=pltpu.VMEM)
    return pl.pallas_call(
        columns_kernel,
        in_specs=[vmem] * 2,
        out_specs=vmem,
        out_shape=jax.ShapeDtypeStruct((parts, units + 8, features // parts), BF16),
        cost_estimate=pl.CostEstimate(flops=0, bytes_accessed=4 * down_weight.size, transcendentals=0),
        name="columns_first",
    )(down_weight, rows)


def swap(array, distance):
    return lax.ppermute(array, "y", [(i, i ^ distance) for i in range(lax.axis_size("y"))])


def exchange(array, axes):
    return lax.all_to_all(array, axes, split_axis=0, concat_axis=0, tiled=True)


def body(
    queries,
    prefix_keys,
    prompt_value_rows,
    generated_keys,
    generated_values,
    suffix_lengths,
    hidden_rows,
    routed_experts,
    routing_weights,
    gate_weight,
    up_weight,
    down_weight,
):
    prompts = lax.axis_size("x")
    own, heads, width = queries.shape[1:]
    scale = width ** (-0.5)

    features = hidden_rows.shape[2]
    quarter = features // prompts
    experts = lax.axis_size(("z", "y", "c")) * gate_weight.shape[0]
    kv = jnp.stack([prefix_keys[0].transpose(1, 0, 2), prompt_value_rows[0].transpose(1, 0, 2)])
    kv, hidden_rows = lax.optimization_barrier((kv, hidden_rows))
    own_columns = columns_first(down_weight[0], hidden_rows[0], prompts)
    kv_all = lax.all_gather(kv, ("z", "c"), axis=0, tiled=False)
    q_pair = jnp.concatenate([queries, swap(queries, NEAR)])

    units = down_weight.shape[1]
    downs = exchange(own_columns, "x")
    row_quarter = downs[:, units : units + own]
    slot, share, suffix_out, suffix_line = local_work(
        scale,
        prompts,
        experts,
        suffix_lengths[0],
        routed_experts,
        routing_weights,
        queries[0],
        generated_keys[0],
        generated_values[0],
    )
    row_quarter, q_pair, slot, share, suffix_out, suffix_line = lax.optimization_barrier(
        (row_quarter, q_pair, slot, share, suffix_out, suffix_line)
    )
    sent = jnp.einsum(
        "rc,rd->cd", slot, row_quarter.reshape(prompts * own, quarter), preferred_element_type=F32
    ).astype(BF16)
    arrived = lax.all_to_all(sent.reshape(experts, SLOTS, quarter), ("z", "y", "c"), split_axis=0, concat_axis=0, tiled=True)
    q_parts = ([swap(q_pair, i) for i in range(NEAR - 1, 0, -1)] + [q_pair])[::-1]
    arrived, q_parts = lax.optimization_barrier((arrived, q_parts))
    pieces = arrived.reshape(experts * SLOTS, quarter)
    pieces = exchange(jnp.broadcast_to(pieces[None], (prompts,) + pieces.shape), "x")
    sums = attention(q_parts, kv_all, scale)
    pieces, sums = lax.optimization_barrier((pieces, sums))
    gathered = lax.all_gather(sums, "y", axis=0, tiled=False)
    acts = exchange(expert_act(pieces, gate_weight[0], up_weight[0]), "x")
    outcome = expert_out(acts, downs, units).reshape(experts, SLOTS, quarter)
    returned = exchange(outcome, ("z", "y", "c")).reshape(experts * SLOTS, quarter)
    mixed = jnp.dot(share, returned, preferred_element_type=F32)
    mixed = (mixed[: prompts * own] + mixed[prompts * own :]).astype(BF16).reshape(prompts, own, quarter)
    mixed = exchange(mixed, "x")
    place = lax.axis_index("y").astype(jnp.int32).reshape(1)
    attended = merge(place, gathered, suffix_out, suffix_line)
    mixed, attended = lax.optimization_barrier((mixed, attended))
    expert_mix = jnp.concatenate([mixed[p] for p in range(prompts)], axis=1)[None]
    attended = attended.reshape(1, own, heads, width)
    return attended, expert_mix


def solution(mesh):
    prompts = mesh.shape["prompt"]
    ctx = mesh.shape["ctx"]
    across = math.isqrt(ctx // 2)
    grid = Mesh(mesh.devices.reshape(prompts, across, across, 2), ("x", "z", "y", "c"))
    lay = ("z", "y", "c")
    placed = (
        P("x", lay, None, None),
        P("x", lay, None, None),
        P("x", lay, None, None),
        P("x", lay, None, None, None),
        P("x", lay, None, None, None),
        P("x", lay),
        P("x", lay, None),
        P(lay, None, None),
        P(lay, None, None),
        P(lay, "x", None),
        P(lay, "x", None),
        P(lay, "x", None),
    )
    return jax.shard_map(
        body,
        mesh=grid,
        in_specs=placed,
        out_specs=(P("x", lay, None, None), P("x", lay, None)),
        check_vma=False,
    )
```
